32 devices in a mesh: group: 1, expert: 32 (over z, y, x, core).
Axes of the slice: x: 2, y: 2, z: 4, core: 2. Of those that a mesh axis runs over, the one named last changes fastest.
Arguments:
- tokens: bfloat16 [4096, 3584], P(('group', 'expert')), may hold values from -6 to 6
- expert_ids: int32 [4096, 8], P(('group', 'expert')), may hold values from 0 to 31, as said below
- route_weight: float32 [4096, 8], P(('group', 'expert')), may hold values from 0.1 to 1
- expert_weight: bfloat16 [32, 3584, 1024], P('expert'), may hold values from -0.09375 to 0.09375
Outputs:
- routed: bfloat16 [4096, 8, 1024], P(('group', 'expert'))
The draws below stay inside these ranges and needn't reach their ends.
Inputs may be any that keep to these rules, and one draw needn't show every extreme that they name: `expert_ids`: each token names 8 different experts; in every group one expert is named by exactly 48 rows of every device; every other expert is named by at most 32 rows of one device, and some expert reaches that.
All inputs are finite; a program needn't handle non-finite values.
Results may differ from the reference program's by a relative error of at most 0.005.
Values may be sent and summed in bfloat16 or wider, within the bound.
A program may use at most 128 MiB of HBM per device.

```python
import math
import jax
import jax.numpy as jnp
from jax import lax

D = 3584
FF = 1024
TOP = 8
TOK_DEV = 128
EXPERTS = 32
TOKENS = 4096
SMALL_CAP = 32
CAP = 48
N_EXPERT = 32


def draw_expert_ids(key, part):
    key = jax.random.fold_in(key, 11)
    hottest = jax.random.randint(jax.random.fold_in(key, 1), (), 0, EXPERTS).astype(jnp.int32)
    block_count = TOKENS // TOK_DEV
    total_picks = TOK_DEV * TOP
    remaining = total_picks - CAP

    def one_block(device):
        block_key = jax.random.fold_in(key, 100 + device)
        shuffled = jax.random.permutation(jax.random.fold_in(block_key, 1), EXPERTS - 1).astype(jnp.int32)
        others = shuffled + (shuffled >= hottest).astype(jnp.int32)
        places = jnp.arange(EXPERTS - 1, dtype=jnp.int32)
        other_counts = jnp.minimum(SMALL_CAP, jnp.maximum(0, remaining - places * SMALL_CAP)).astype(jnp.int32)
        listing = jnp.concatenate([hottest[None], others])
        counts = jnp.concatenate([jnp.full((1,), CAP, jnp.int32), other_counts])
        ends = jnp.cumsum(counts).astype(jnp.int32)
        spots = jnp.arange(total_picks, dtype=jnp.int32)
        which = jnp.searchsorted(ends, spots, side='right').astype(jnp.int32)
        sequence = listing[which]
        table = sequence.reshape(TOP, TOK_DEV).T
        row_order = jax.random.permutation(jax.random.fold_in(block_key, 2), TOK_DEV).astype(jnp.int32)
        table = table[row_order]
        row_keys = jax.random.split(jax.random.fold_in(block_key, 3), TOK_DEV)
        column_orders = jax.vmap(lambda k: jax.random.permutation(k, TOP).astype(jnp.int32))(row_keys)
        return jnp.take_along_axis(table, column_orders, axis=1)
    blocks = jax.vmap(one_block)(jnp.arange(block_count, dtype=jnp.int32))
    return blocks.reshape(TOKENS, TOP).astype(jnp.int32)


def level_of(own_key, dims, pieces, least, largest):
    level, own = 1.0, jax.random.fold_in(own_key, 6)
    for position, parts in pieces:
        heights = jnp.exp(jax.random.uniform(jax.random.fold_in(own, position), (parts,), jnp.float32, least / len(pieces), largest / len(pieces)))
        level = level * jnp.repeat(heights, dims[position] // parts).reshape([-1 if axis == position else 1 for axis in range(len(dims))])
    return level


def normal_values(stream_key, extent, scale, most, shards=(), kind=jnp.bfloat16):
    array = jax.random.normal(stream_key, extent, jnp.float32) * scale
    if len(shards) > 0:
        array = level_of(stream_key, extent, shards, -0.22, 0.18) * array
    return jnp.clip(array, min=-most, max=most).astype(kind)


def setup_inputs(seed: int = 0, part: int = 0) -> dict:
    key_list = jax.random.split(jax.random.key(seed), 5)
    part_keys = jax.random.split(jax.random.fold_in(key_list[4], part), 5)
    tokens = normal_values(part_keys[0], (TOKENS, D), 1.0, 6.0, ((0, 32),))
    expert_ids = draw_expert_ids(jax.random.fold_in(jax.random.fold_in(key_list[4], part), 71), part)
    route_weight = jnp.clip(jnp.exp(math.log(1.0) - 2.3025851 * jax.random.uniform(part_keys[2], (TOKENS, TOP), jnp.float32) ** level_of(part_keys[2], (TOKENS, TOP), ((0, 32),), -0.2, 0.2)), 0.1, 1.0)
    expert_weight = normal_values(key_list[3], (EXPERTS, D, FF), D ** -0.5, 0.09375, ((0, 32),))
    return {"tokens": tokens, "expert_ids": expert_ids, "route_weight": route_weight, "expert_weight": expert_weight}


def reference(tokens, expert_ids, route_weight, expert_weight):
    flat_ids = expert_ids.reshape(-1)
    slot_total = flat_ids.shape[0]
    row_limit = N_EXPERT * CAP

    def per_expert(buffer, expert):
        found = jnp.nonzero(flat_ids == expert, size=row_limit, fill_value=slot_total)[0]
        token_rows = tokens[jnp.minimum(found, slot_total - 1) // TOP]
        weight = lax.dynamic_index_in_dim(expert_weight, expert, 0, keepdims=False)
        activated = jax.nn.silu(jnp.dot(token_rows, weight, preferred_element_type=jnp.float32)).astype(jnp.bfloat16)
        buffer = buffer.at[found].set(activated, mode="drop")
        return buffer, None

    start = jnp.zeros((slot_total, FF), jnp.bfloat16)
    buffer, _ = lax.scan(per_expert, start, jnp.arange(EXPERTS, dtype=jnp.int32))
    routed = route_weight.reshape(-1, 1) * buffer.astype(jnp.float32)
    return routed.astype(jnp.bfloat16).reshape(TOKENS, TOP, FF)
```

```python
import jax
import jax.numpy as jnp
from jax import lax
from jax.experimental import pallas as pl
from jax.experimental.pallas import tpu as pltpu
from jax.sharding import PartitionSpec as P

MESH = pl.DeviceIdType.MESH
DEPTH = 4
PLANE = 8
COLS = 256


def slots(expert_ids, experts, capacity):
    columns = jnp.arange(experts, dtype=jnp.int32)
    named = expert_ids[:, :, None] == columns[None, None, :]
    mask = jnp.any(named, axis=1)
    rows = jnp.arange(expert_ids.shape[0], dtype=jnp.int32)
    earlier = (rows[None, :] < rows[:, None]).astype(jnp.bfloat16)
    rank = jnp.dot(earlier, mask.astype(jnp.bfloat16), preferred_element_type=jnp.float32)
    rank = rank.astype(jnp.int32)
    masked = jnp.where(mask, rank, -1)
    places = jnp.arange(capacity, dtype=jnp.int32)
    chooser = (masked.T[:, None, :] == places[None, :, None]).astype(jnp.bfloat16)
    picked = jnp.sum(jnp.where(named, rank[:, None, :], 0), axis=2)
    return chooser, expert_ids * capacity + picked


def exchange_kernel(
    tokens, chooser, weight, res, held, wv, selr, packed, outs,
    own_sem, w_sem, sel_send, sel_recv, send_sem, recv_sem, out_send, out_recv,
):
    me = lax.axis_index("expert")
    devices = held.shape[0]
    half = held.shape[1] // 2
    z = me // PLANE
    spot = lax.rem(me, PLANE)
    core = lax.rem(spot, 2)
    x = lax.rem(spot // 2, 2)
    y = spot // 4
    sib = me + 1 - 2 * core
    xn = me + 2 * (1 - 2 * x)
    yn = me + 4 * (1 - 2 * y)
    diag = 4 * (1 - 2 * y) + 2 * (1 - 2 * x)

    weight_copy = pltpu.make_async_copy(weight.at[0], wv, w_sem)
    weight_copy.start()
    own_copy = pltpu.make_async_copy(tokens, held.at[me], own_sem.at[0])
    own_copy.start()
    sel_copy = pltpu.make_async_copy(chooser.at[me], selr.at[me], own_sem.at[1])
    sel_copy.start()

    barrier = pltpu.get_barrier_semaphore()

    @pl.loop(1, devices)
    def _(d):
        pl.semaphore_signal(
            barrier, inc=1, device_id={"expert": lax.rem(me + d, devices)}, device_id_type=MESH
        )

    pl.semaphore_wait(barrier, devices - 1)
    own_copy.wait()
    sel_copy.wait()

    def sel_to(d):
        to = lax.rem(me + d, devices)
        return pltpu.make_async_remote_copy(
            src_ref=chooser.at[to], dst_ref=selr.at[me],
            send_sem=sel_send.at[to], recv_sem=sel_recv.at[me],
            device_id={"expert": to}, device_id_type=MESH,
        )

    def piece(block, h, to, index):
        part = held.at[block, pl.ds(h * half, half)]
        return pltpu.make_async_remote_copy(
            src_ref=part, dst_ref=part,
            send_sem=send_sem.at[index], recv_sem=recv_sem.at[block, h],
            device_id={"expert": to}, device_id_type=MESH,
        )

    sent = []

    def send(block, h, to, when=None):
        copy = piece(block, h, to, len(sent))
        if when is None:
            copy.start()
        else:
            pl.when(when)(copy.start)
        sent.append((copy, when))

    def arrived(block, h):
        piece(block, h, sib, 0).wait_recv()

    upper = z // 2
    mirrored = z + upper * (3 - 2 * z)

    def plane(t):
        order = t + mirrored * (1 - 2 * t) if t < 2 else t
        return order + upper * (3 - 2 * order)

    def base(t):
        return plane(t) * PLANE

    def stage_a(t):
        block, level = base(t) + spot, plane(t)
        for h in (0, 1):
            if t > 0:
                arrived(block, h)
            send(block, h, lax.rem(me + PLANE, devices),
                 jnp.logical_and(z < DEPTH - 1, level <= z))
            send(block, h, lax.rem(me + devices - PLANE, devices),
                 jnp.logical_and(z > 0, level >= z))
            send(block, h, (xn, yn)[h])
        for h in (0, 1):
            send(block, h, (yn, xn)[h])
            send(block, h, sib)

    def stage_b(t):
        for h, near, to in ((0, xn, yn), (1, yn, xn)):
            block = base(t) + lax.rem(near, PLANE)
            arrived(block, h)
            send(block, h, to)
            send(block, h, sib)

    def stage_c(t):
        across = base(t) + spot + diag
        for block, h in (
            (base(t) + lax.rem(yn, PLANE), 0), (base(t) + lax.rem(xn, PLANE), 1),
            (across, 0), (across, 1),
        ):
            arrived(block, h)
            send(block, h, sib)

    def out_to(s):
        return pltpu.make_async_remote_copy(
            src_ref=outs.at[s], dst_ref=res.at[me],
            send_sem=out_send.at[s], recv_sem=out_recv.at[me],
            device_id={"expert": s}, device_id_type=MESH,
        )

    cap = selr.shape[1]

    def stage_d(t):
        first = base(t)
        for q in range(4):
            for h in (0, 1):
                arrived(first + 2 * q + (1 - core), h)

        @pl.loop(0, PLANE)
        def _(q):
            s = first + q

            @pl.when(s != me)
            def _():
                pltpu.make_async_remote_copy(
                    src_ref=chooser.at[s], dst_ref=selr.at[s],
                    send_sem=sel_send.at[s], recv_sem=sel_recv.at[s],
                    device_id={"expert": sib}, device_id_type=MESH,
                ).wait_recv()

            rows = pl.ds(pl.multiple_of(q * cap, 16), cap)
            packed[rows, :] = jnp.dot(
                selr[s], held[s], preferred_element_type=jnp.float32
            ).astype(jnp.bfloat16)

        if t == 0:
            weight_copy.wait()

        @pl.loop(0, wv.shape[1] // COLS)
        def _(j):
            columns = pl.ds(pl.multiple_of(j * COLS, COLS), COLS)
            v = jnp.dot(packed[...], wv[:, columns], preferred_element_type=jnp.float32)
            act = (v / (1.0 + jnp.exp(-v))).astype(jnp.bfloat16)
            outs[pl.ds(first, PLANE), :, columns] = act.reshape(PLANE, cap, COLS)

        @pl.loop(0, PLANE)
        def _(q):
            s = first + q

            @pl.when(s != me)
            def _():
                out_to(s).start()

            @pl.when(s == me)
            def _():
                pltpu.make_async_copy(outs.at[me], res.at[me], own_sem.at[2]).start()

    stage_a(0)

    @pl.loop(1, devices)
    def _(d):
        sel_to(d).start()

    stage_b(0)
    stage_a(1)
    stage_c(0)
    stage_b(1)
    stage_a(2)
    stage_d(0)
    stage_c(1)
    stage_b(2)
    stage_a(3)
    stage_d(1)
    stage_c(2)
    stage_b(3)
    stage_d(2)
    stage_c(3)
    stage_d(3)

    for copy, when in sent:
        if when is None:
            copy.wait_send()
        else:
            pl.when(when)(copy.wait_send)

    @pl.loop(1, devices)
    def _(d):
        sel_to(d).wait_send()
        s = lax.rem(me + d, devices)
        out_to(s).wait_send()
        pltpu.make_async_remote_copy(
            src_ref=outs.at[s], dst_ref=res.at[s],
            send_sem=out_send.at[s], recv_sem=out_recv.at[s],
            device_id={"expert": s}, device_id_type=MESH,
        ).wait_recv()

    pltpu.make_async_copy(outs.at[me], res.at[me], own_sem.at[2]).wait()


def exchange(tokens, chooser, weight):
    rows, model_width = tokens.shape
    devices, capacity, _ = chooser.shape
    hidden = weight.shape[2]
    sends = 22 * DEPTH
    anywhere = pl.BlockSpec(memory_space=pl.ANY)
    return pl.pallas_call(
        exchange_kernel,
        out_shape=jax.ShapeDtypeStruct((devices, capacity, hidden), jnp.bfloat16),
        in_specs=[anywhere, pl.BlockSpec(memory_space=pltpu.VMEM), anywhere],
        out_specs=anywhere,
        scratch_shapes=[
            pltpu.VMEM((devices, rows, model_width), jnp.bfloat16),
            pltpu.VMEM((model_width, hidden), jnp.bfloat16),
            pltpu.VMEM((devices, capacity, rows), jnp.bfloat16),
            pltpu.VMEM((PLANE * capacity, model_width), jnp.bfloat16),
            pltpu.VMEM((devices, capacity, hidden), jnp.bfloat16),
            pltpu.SemaphoreType.DMA((3,)),
            pltpu.SemaphoreType.DMA,
            pltpu.SemaphoreType.DMA((devices,)),
            pltpu.SemaphoreType.DMA((devices,)),
            pltpu.SemaphoreType.DMA((sends,)),
            pltpu.SemaphoreType.DMA((devices, 2)),
            pltpu.SemaphoreType.DMA((devices,)),
            pltpu.SemaphoreType.DMA((devices,)),
        ],
        compiler_params=pltpu.CompilerParams(
            collective_id=0, has_side_effects=True, vmem_limit_bytes=56 * 1024 * 1024
        ),
    )(tokens, chooser, weight)


def body(tokens, expert_ids, route_weight, expert_weight):
    tok_rows, picks = expert_ids.shape
    per_device, model_width, hidden = expert_weight.shape
    devices = lax.axis_size("expert")
    experts = per_device * devices
    small_cap = (tok_rows * picks + experts - 1) // experts
    capacity = max(small_cap + 1, small_cap + small_cap // 2)
    chooser, place = slots(expert_ids, experts, capacity)
    if devices == DEPTH * PLANE and per_device == 1 and lax.axis_size("group") == 1:
        results = exchange(tokens, chooser, expert_weight)
    else:
        packed = jnp.dot(
            chooser.reshape(experts * capacity, tok_rows), tokens,
            preferred_element_type=jnp.float32,
        ).astype(jnp.bfloat16).reshape(experts, capacity, model_width)
        received = lax.all_to_all(packed, "expert", split_axis=0, concat_axis=0, tiled=True)
        grouped = received.reshape(devices, per_device, capacity, model_width)
        preact = jnp.einsum(
            "necd,edf->necf", grouped, expert_weight, preferred_element_type=jnp.float32
        )
        activated = jax.nn.silu(preact).astype(jnp.bfloat16).reshape(experts, capacity, hidden)
        results = lax.all_to_all(activated, "expert", split_axis=0, concat_axis=0, tiled=True)
    positions = jnp.arange(experts * capacity, dtype=jnp.int32)
    finder = (place.reshape(-1, 1) == positions[None, :]).astype(jnp.bfloat16)
    gathered = jnp.dot(
        finder, results.reshape(experts * capacity, hidden), preferred_element_type=jnp.float32
    )
    routed = route_weight.reshape(-1, 1) * gathered
    return routed.astype(jnp.bfloat16).reshape(tok_rows, picks, hidden)


def solution(mesh):
    in_specs = (
        P(("group", "expert"), None),
        P(("group", "expert"), None),
        P(("group", "expert"), None),
        P("expert", None, None),
    )
    out_specs = P(("group", "expert"), None, None)
    return jax.shard_map(body, mesh=mesh, in_specs=in_specs, out_specs=out_specs, check_vma=False)
```

```python
import jax
import jax.numpy as jnp
from jax import lax
from jax.experimental import pallas as pl
from jax.experimental.pallas import tpu as pltpu
from jax.sharding import PartitionSpec as P

MESH = pl.DeviceIdType.MESH
DEPTH = 4
PLANE = 8
COLS = 256


def slots(expert_ids, experts, capacity):
    columns = jnp.arange(experts, dtype=jnp.int32)
    named = expert_ids[:, :, None] == columns[None, None, :]
    mask = jnp.any(named, axis=1)
    rows = jnp.arange(expert_ids.shape[0], dtype=jnp.int32)
    earlier = (rows[None, :] < rows[:, None]).astype(jnp.bfloat16)
    rank = jnp.dot(earlier, mask.astype(jnp.bfloat16), preferred_element_type=jnp.float32)
    rank = rank.astype(jnp.int32)
    masked = jnp.where(mask, rank, -1)
    places = jnp.arange(capacity, dtype=jnp.int32)
    chooser = (masked.T[:, None, :] == places[None, :, None]).astype(jnp.bfloat16)
    picked = jnp.sum(jnp.where(named, rank[:, None, :], 0), axis=2)
    return chooser, expert_ids * capacity + picked


def exchange_kernel(
    tokens, chooser, weight, res, held, wv, selr, packed, outs,
    own_sem, w_sem, sel_send, sel_recv, send_sem, recv_sem, out_send, out_recv,
):
    me = lax.axis_index("expert")
    devices = held.shape[0]
    half = held.shape[1] // 2
    z = me // PLANE
    spot = lax.rem(me, PLANE)
    core = lax.rem(spot, 2)
    x = lax.rem(spot // 2, 2)
    y = spot // 4
    sib = me + 1 - 2 * core
    xn = me + 2 * (1 - 2 * x)
    yn = me + 4 * (1 - 2 * y)
    diag = 4 * (1 - 2 * y) + 2 * (1 - 2 * x)

    weight_copy = pltpu.make_async_copy(weight.at[0], wv, w_sem)
    weight_copy.start()
    own_copy = pltpu.make_async_copy(tokens, held.at[me], own_sem.at[0])
    own_copy.start()
    sel_copy = pltpu.make_async_copy(chooser.at[me], selr.at[me], own_sem.at[1])
    sel_copy.start()

    barrier = pltpu.get_barrier_semaphore()

    @pl.loop(1, devices)
    def _(d):
        pl.semaphore_signal(
            barrier, inc=1, device_id={"expert": lax.rem(me + d, devices)}, device_id_type=MESH
        )

    pl.semaphore_wait(barrier, devices - 1)
    own_copy.wait()
    sel_copy.wait()

    def sel_to(d):
        to = lax.rem(me + d, devices)
        return pltpu.make_async_remote_copy(
            src_ref=chooser.at[to], dst_ref=selr.at[me],
            send_sem=sel_send.at[to], recv_sem=sel_recv.at[me],
            device_id={"expert": to}, device_id_type=MESH,
        )

    def piece(block, h, to, index):
        part = held.at[block, pl.ds(h * half, half)]
        return pltpu.make_async_remote_copy(
            src_ref=part, dst_ref=part,
            send_sem=send_sem.at[index], recv_sem=recv_sem.at[block, h],
            device_id={"expert": to}, device_id_type=MESH,
        )

    sent = []

    def send(block, h, to, when=None):
        copy = piece(block, h, to, len(sent))
        if when is None:
            copy.start()
        else:
            pl.when(when)(copy.start)
        sent.append((copy, when))

    def arrived(block, h):
        piece(block, h, sib, 0).wait_recv()

    upper = z // 2
    mirrored = z + upper * (3 - 2 * z)

    def plane(t):
        order = t + mirrored * (1 - 2 * t) if t < 2 else t
        return order + upper * (3 - 2 * order)

    def base(t):
        return plane(t) * PLANE

    def stage_a(t):
        block, level = base(t) + spot, plane(t)
        for h in (0, 1):
            if t > 0:
                arrived(block, h)
            send(block, h, lax.rem(me + PLANE, devices),
                 jnp.logical_and(z < DEPTH - 1, level <= z))
            send(block, h, lax.rem(me + devices - PLANE, devices),
                 jnp.logical_and(z > 0, level >= z))
            send(block, h, (xn, yn)[h])
        for h in (0, 1):
            send(block, h, (yn, xn)[h])
            send(block, h, sib)

    def stage_b(t):
        for h, near, to in ((0, xn, yn), (1, yn, xn)):
            block = base(t) + lax.rem(near, PLANE)
            arrived(block, h)
            send(block, h, to)
            send(block, h, sib)

    def stage_c(t):
        across = base(t) + spot + diag
        for block, h in (
            (base(t) + lax.rem(yn, PLANE), 0), (base(t) + lax.rem(xn, PLANE), 1),
            (across, 0), (across, 1),
        ):
            arrived(block, h)
            send(block, h, sib)

    def out_to(s):
        return pltpu.make_async_remote_copy(
            src_ref=outs.at[s], dst_ref=res.at[me],
            send_sem=out_send.at[s], recv_sem=out_recv.at[me],
            device_id={"expert": s}, device_id_type=MESH,
        )

    cap = selr.shape[1]

    def stage_d(t):
        first = base(t)
        for q in range(4):
            for h in (0, 1):
                arrived(first + 2 * q + (1 - core), h)

        @pl.loop(0, PLANE)
        def _(q):
            s = first + q

            @pl.when(s != me)
            def _():
                pltpu.make_async_remote_copy(
                    src_ref=chooser.at[s], dst_ref=selr.at[s],
                    send_sem=sel_send.at[s], recv_sem=sel_recv.at[s],
                    device_id={"expert": sib}, device_id_type=MESH,
                ).wait_recv()

            rows = pl.ds(pl.multiple_of(q * cap, 16), cap)
            packed[rows, :] = jnp.dot(
                selr[s], held[s], preferred_element_type=jnp.float32
            ).astype(jnp.bfloat16)

        if t == 0:
            weight_copy.wait()

        @pl.loop(0, wv.shape[1] // COLS)
        def _(j):
            columns = pl.ds(pl.multiple_of(j * COLS, COLS), COLS)
            v = jnp.dot(packed[...], wv[:, columns], preferred_element_type=jnp.float32)
            act = (v / (1.0 + jnp.exp(-v))).astype(jnp.bfloat16)
            outs[pl.ds(first, PLANE), :, columns] = act.reshape(PLANE, cap, COLS)


    def send_out(t):
        first = base(t)

        @pl.loop(0, PLANE)
        def _(q):
            s = first + lax.rem(spot + q, PLANE)

            @pl.when(s != me)
            def _():
                out_to(s).start()

            @pl.when(s == me)
            def _():
                pltpu.make_async_copy(outs.at[me], res.at[me], own_sem.at[2]).start()

    stage_a(0)

    @pl.loop(1, devices)
    def _(d):
        sel_to(d).start()

    stage_b(0)
    stage_a(1)
    stage_c(0)
    stage_b(1)
    stage_a(2)
    stage_d(0)
    stage_c(1)
    stage_b(2)
    stage_a(3)
    stage_d(1)
    send_out(1)
    stage_c(2)
    stage_b(3)
    stage_d(2)
    send_out(2)
    stage_c(3)
    stage_d(3)
    send_out(3)
    send_out(0)

    for copy, when in sent:
        if when is None:
            copy.wait_send()
        else:
            pl.when(when)(copy.wait_send)

    @pl.loop(1, devices)
    def _(d):
        sel_to(d).wait_send()
        s = lax.rem(me + d, devices)
        out_to(s).wait_send()
        pltpu.make_async_remote_copy(
            src_ref=outs.at[s], dst_ref=res.at[s],
            send_sem=out_send.at[s], recv_sem=out_recv.at[s],
            device_id={"expert": s}, device_id_type=MESH,
        ).wait_recv()

    pltpu.make_async_copy(outs.at[me], res.at[me], own_sem.at[2]).wait()


def exchange(tokens, chooser, weight):
    rows, model_width = tokens.shape
    devices, capacity, _ = chooser.shape
    hidden = weight.shape[2]
    sends = 22 * DEPTH
    anywhere = pl.BlockSpec(memory_space=pl.ANY)
    return pl.pallas_call(
        exchange_kernel,
        out_shape=jax.ShapeDtypeStruct((devices, capacity, hidden), jnp.bfloat16),
        in_specs=[anywhere, pl.BlockSpec(memory_space=pltpu.VMEM), anywhere],
        out_specs=anywhere,
        scratch_shapes=[
            pltpu.VMEM((devices, rows, model_width), jnp.bfloat16),
            pltpu.VMEM((model_width, hidden), jnp.bfloat16),
            pltpu.VMEM((devices, capacity, rows), jnp.bfloat16),
            pltpu.VMEM((PLANE * capacity, model_width), jnp.bfloat16),
            pltpu.VMEM((devices, capacity, hidden), jnp.bfloat16),
            pltpu.SemaphoreType.DMA((3,)),
            pltpu.SemaphoreType.DMA,
            pltpu.SemaphoreType.DMA((devices,)),
            pltpu.SemaphoreType.DMA((devices,)),
            pltpu.SemaphoreType.DMA((sends,)),
            pltpu.SemaphoreType.DMA((devices, 2)),
            pltpu.SemaphoreType.DMA((devices,)),
            pltpu.SemaphoreType.DMA((devices,)),
        ],
        compiler_params=pltpu.CompilerParams(
            collective_id=0, has_side_effects=True, vmem_limit_bytes=56 * 1024 * 1024
        ),
    )(tokens, chooser, weight)


def body(tokens, expert_ids, route_weight, expert_weight):
    tok_rows, picks = expert_ids.shape
    per_device, model_width, hidden = expert_weight.shape
    devices = lax.axis_size("expert")
    experts = per_device * devices
    small_cap = (tok_rows * picks + experts - 1) // experts
    capacity = max(small_cap + 1, small_cap + small_cap // 2)
    chooser, place = slots(expert_ids, experts, capacity)
    if devices == DEPTH * PLANE and per_device == 1 and lax.axis_size("group") == 1:
        results = exchange(tokens, chooser, expert_weight)
    else:
        packed = jnp.dot(
            chooser.reshape(experts * capacity, tok_rows), tokens,
            preferred_element_type=jnp.float32,
        ).astype(jnp.bfloat16).reshape(experts, capacity, model_width)
        received = lax.all_to_all(packed, "expert", split_axis=0, concat_axis=0, tiled=True)
        grouped = received.reshape(devices, per_device, capacity, model_width)
        preact = jnp.einsum(
            "necd,edf->necf", grouped, expert_weight, preferred_element_type=jnp.float32
        )
        activated = jax.nn.silu(preact).astype(jnp.bfloat16).reshape(experts, capacity, hidden)
        results = lax.all_to_all(activated, "expert", split_axis=0, concat_axis=0, tiled=True)
    positions = jnp.arange(experts * capacity, dtype=jnp.int32)
    finder = (place.reshape(-1, 1) == positions[None, :]).astype(jnp.bfloat16)
    gathered = jnp.dot(
        finder, results.reshape(experts * capacity, hidden), preferred_element_type=jnp.float32
    )
    routed = route_weight.reshape(-1, 1) * gathered
    return routed.astype(jnp.bfloat16).reshape(tok_rows, picks, hidden)


def solution(mesh):
    in_specs = (
        P(("group", "expert"), None),
        P(("group", "expert"), None),
        P(("group", "expert"), None),
        P("expert", None, None),
    )
    out_specs = P(("group", "expert"), None, None)
    return jax.shard_map(body, mesh=mesh, in_specs=in_specs, out_specs=out_specs, check_vma=False)
```

```python
import jax
import jax.numpy as jnp
from jax import lax
from jax.experimental import pallas as pl
from jax.experimental.pallas import tpu as pltpu
from jax.sharding import PartitionSpec as P

MESH = pl.DeviceIdType.MESH
DEPTH = 4
PLANE = 8
COLS = 256


def slots(expert_ids, experts, capacity):
    columns = jnp.arange(experts, dtype=jnp.int32)
    named = expert_ids[:, :, None] == columns[None, None, :]
    mask = jnp.any(named, axis=1)
    rows = jnp.arange(expert_ids.shape[0], dtype=jnp.int32)
    earlier = (rows[None, :] < rows[:, None]).astype(jnp.bfloat16)
    rank = jnp.dot(earlier, mask.astype(jnp.bfloat16), preferred_element_type=jnp.float32)
    rank = rank.astype(jnp.int32)
    masked = jnp.where(mask, rank, -1)
    places = jnp.arange(capacity, dtype=jnp.int32)
    chooser = (masked.T[:, None, :] == places[None, :, None]).astype(jnp.bfloat16)
    picked = jnp.sum(jnp.where(named, rank[:, None, :], 0), axis=2)
    return chooser, expert_ids * capacity + picked


def exchange_kernel(
    tokens, chooser, weight, res, held, wv, selr, packed, outs,
    own_sem, w_sem, sel_send, sel_recv, send_sem, recv_sem, out_send, out_recv,
):
    me = lax.axis_index("expert")
    devices = held.shape[0]
    half = held.shape[1] // 2
    z = me // PLANE
    spot = lax.rem(me, PLANE)
    core = lax.rem(spot, 2)
    x = lax.rem(spot // 2, 2)
    y = spot // 4
    sib = me + 1 - 2 * core
    xn = me + 2 * (1 - 2 * x)
    yn = me + 4 * (1 - 2 * y)
    diag = 4 * (1 - 2 * y) + 2 * (1 - 2 * x)

    weight_copy = pltpu.make_async_copy(weight.at[0], wv, w_sem)
    weight_copy.start()
    own_copy = pltpu.make_async_copy(tokens, held.at[me], own_sem.at[0])
    own_copy.start()
    sel_copy = pltpu.make_async_copy(chooser.at[me], selr.at[me], own_sem.at[1])
    sel_copy.start()

    barrier = pltpu.get_barrier_semaphore()

    @pl.loop(1, devices)
    def _(d):
        pl.semaphore_signal(
            barrier, inc=1, device_id={"expert": lax.rem(me + d, devices)}, device_id_type=MESH
        )

    pl.semaphore_wait(barrier, devices - 1)
    own_copy.wait()
    sel_copy.wait()

    def sel_to(d):
        to = lax.rem(me + d, devices)
        return pltpu.make_async_remote_copy(
            src_ref=chooser.at[to], dst_ref=selr.at[me],
            send_sem=sel_send.at[to], recv_sem=sel_recv.at[me],
            device_id={"expert": to}, device_id_type=MESH,
        )

    def piece(block, h, to, index):
        part = held.at[block, pl.ds(h * half, half)]
        return pltpu.make_async_remote_copy(
            src_ref=part, dst_ref=part,
            send_sem=send_sem.at[index], recv_sem=recv_sem.at[block, h],
            device_id={"expert": to}, device_id_type=MESH,
        )

    sent = []

    def send(block, h, to, when=None):
        copy = piece(block, h, to, len(sent))
        if when is None:
            copy.start()
        else:
            pl.when(when)(copy.start)
        sent.append((copy, when))

    def arrived(block, h):
        piece(block, h, sib, 0).wait_recv()

    upper = z // 2
    mirrored = z + upper * (3 - 2 * z)

    def plane(t):
        order = t + mirrored * (1 - 2 * t) if t < 2 else t
        return order + upper * (3 - 2 * order)

    def base(t):
        return plane(t) * PLANE

    def stage_a(t):
        block, level = base(t) + spot, plane(t)
        for h in (0, 1):
            if t > 0:
                arrived(block, h)
            send(block, h, lax.rem(me + PLANE, devices),
                 jnp.logical_and(z < DEPTH - 1, level <= z))
            send(block, h, lax.rem(me + devices - PLANE, devices),
                 jnp.logical_and(z > 0, level >= z))
            send(block, h, (xn, yn)[h])
        for h in (0, 1):
            send(block, h, (yn, xn)[h])
            send(block, h, sib)

    def stage_b(t):
        for h, near, to in ((0, xn, yn), (1, yn, xn)):
            block = base(t) + lax.rem(near, PLANE)
            arrived(block, h)
            send(block, h, to)
            send(block, h, sib)

    def stage_c(t):
        across = base(t) + spot + diag
        for block, h in (
            (base(t) + lax.rem(yn, PLANE), 0), (base(t) + lax.rem(xn, PLANE), 1),
            (across, 0), (across, 1),
        ):
            arrived(block, h)
            send(block, h, sib)

    def out_to(s):
        return pltpu.make_async_remote_copy(
            src_ref=outs.at[s], dst_ref=res.at[me],
            send_sem=out_send.at[s], recv_sem=out_recv.at[me],
            device_id={"expert": s}, device_id_type=MESH,
        )

    cap = selr.shape[1]

    def stage_d(t):
        first = base(t)
        for q in range(4):
            for h in (0, 1):
                arrived(first + 2 * q + (1 - core), h)

        @pl.loop(0, PLANE)
        def _(q):
            s = first + q

            @pl.when(s != me)
            def _():
                pltpu.make_async_remote_copy(
                    src_ref=chooser.at[s], dst_ref=selr.at[s],
                    send_sem=sel_send.at[s], recv_sem=sel_recv.at[s],
                    device_id={"expert": sib}, device_id_type=MESH,
                ).wait_recv()

            rows = pl.ds(pl.multiple_of(q * cap, 16), cap)
            packed[rows, :] = jnp.dot(
                selr[s], held[s], preferred_element_type=jnp.float32
            ).astype(jnp.bfloat16)

        if t == 1:
            weight_copy.wait()

        @pl.loop(0, wv.shape[1] // COLS)
        def _(j):
            columns = pl.ds(pl.multiple_of(j * COLS, COLS), COLS)
            v = jnp.dot(packed[...], wv[:, columns], preferred_element_type=jnp.float32)
            act = (v / (1.0 + jnp.exp(-v))).astype(jnp.bfloat16)
            outs[pl.ds(first, PLANE), :, columns] = act.reshape(PLANE, cap, COLS)


    def send_out(t):
        first = base(t)

        @pl.loop(0, PLANE)
        def _(q):
            s = first + lax.rem(spot + q, PLANE)

            @pl.when(s != me)
            def _():
                out_to(s).start()

            @pl.when(s == me)
            def _():
                pltpu.make_async_copy(outs.at[me], res.at[me], own_sem.at[2]).start()

    stage_a(0)

    @pl.loop(1, devices)
    def _(d):
        sel_to(d).start()

    stage_b(0)
    stage_a(1)
    stage_c(0)
    stage_b(1)
    stage_a(2)
    stage_c(1)
    stage_b(2)
    stage_a(3)
    stage_d(1)
    send_out(1)
    stage_c(2)
    stage_d(2)
    send_out(2)
    stage_b(3)
    stage_d(0)
    stage_c(3)
    stage_d(3)
    send_out(3)
    send_out(0)

    for copy, when in sent:
        if when is None:
            copy.wait_send()
        else:
            pl.when(when)(copy.wait_send)

    @pl.loop(1, devices)
    def _(d):
        sel_to(d).wait_send()
        s = lax.rem(me + d, devices)
        out_to(s).wait_send()
        pltpu.make_async_remote_copy(
            src_ref=outs.at[s], dst_ref=res.at[s],
            send_sem=out_send.at[s], recv_sem=out_recv.at[s],
            device_id={"expert": s}, device_id_type=MESH,
        ).wait_recv()

    pltpu.make_async_copy(outs.at[me], res.at[me], own_sem.at[2]).wait()


def exchange(tokens, chooser, weight):
    rows, model_width = tokens.shape
    devices, capacity, _ = chooser.shape
    hidden = weight.shape[2]
    sends = 22 * DEPTH
    anywhere = pl.BlockSpec(memory_space=pl.ANY)
    return pl.pallas_call(
        exchange_kernel,
        out_shape=jax.ShapeDtypeStruct((devices, capacity, hidden), jnp.bfloat16),
        in_specs=[anywhere, pl.BlockSpec(memory_space=pltpu.VMEM), anywhere],
        out_specs=anywhere,
        scratch_shapes=[
            pltpu.VMEM((devices, rows, model_width), jnp.bfloat16),
            pltpu.VMEM((model_width, hidden), jnp.bfloat16),
            pltpu.VMEM((devices, capacity, rows), jnp.bfloat16),
            pltpu.VMEM((PLANE * capacity, model_width), jnp.bfloat16),
            pltpu.VMEM((devices, capacity, hidden), jnp.bfloat16),
            pltpu.SemaphoreType.DMA((3,)),
            pltpu.SemaphoreType.DMA,
            pltpu.SemaphoreType.DMA((devices,)),
            pltpu.SemaphoreType.DMA((devices,)),
            pltpu.SemaphoreType.DMA((sends,)),
            pltpu.SemaphoreType.DMA((devices, 2)),
            pltpu.SemaphoreType.DMA((devices,)),
            pltpu.SemaphoreType.DMA((devices,)),
        ],
        compiler_params=pltpu.CompilerParams(
            collective_id=0, has_side_effects=True, vmem_limit_bytes=56 * 1024 * 1024
        ),
    )(tokens, chooser, weight)


def body(tokens, expert_ids, route_weight, expert_weight):
    tok_rows, picks = expert_ids.shape
    per_device, model_width, hidden = expert_weight.shape
    devices = lax.axis_size("expert")
    experts = per_device * devices
    small_cap = (tok_rows * picks + experts - 1) // experts
    capacity = max(small_cap + 1, small_cap + small_cap // 2)
    chooser, place = slots(expert_ids, experts, capacity)
    if devices == DEPTH * PLANE and per_device == 1 and lax.axis_size("group") == 1:
        results = exchange(tokens, chooser, expert_weight)
    else:
        packed = jnp.dot(
            chooser.reshape(experts * capacity, tok_rows), tokens,
            preferred_element_type=jnp.float32,
        ).astype(jnp.bfloat16).reshape(experts, capacity, model_width)
        received = lax.all_to_all(packed, "expert", split_axis=0, concat_axis=0, tiled=True)
        grouped = received.reshape(devices, per_device, capacity, model_width)
        preact = jnp.einsum(
            "necd,edf->necf", grouped, expert_weight, preferred_element_type=jnp.float32
        )
        activated = jax.nn.silu(preact).astype(jnp.bfloat16).reshape(experts, capacity, hidden)
        results = lax.all_to_all(activated, "expert", split_axis=0, concat_axis=0, tiled=True)
    positions = jnp.arange(experts * capacity, dtype=jnp.int32)
    finder = (place.reshape(-1, 1) == positions[None, :]).astype(jnp.bfloat16)
    gathered = jnp.dot(
        finder, results.reshape(experts * capacity, hidden), preferred_element_type=jnp.float32
    )
    routed = route_weight.reshape(-1, 1) * gathered
    return routed.astype(jnp.bfloat16).reshape(tok_rows, picks, hidden)


def solution(mesh):
    in_specs = (
        P(("group", "expert"), None),
        P(("group", "expert"), None),
        P(("group", "expert"), None),
        P("expert", None, None),
    )
    out_specs = P(("group", "expert"), None, None)
    return jax.shard_map(body, mesh=mesh, in_specs=in_specs, out_specs=out_specs, check_vma=False)
```

```python
import jax
import jax.numpy as jnp
from jax import lax
from jax.experimental import pallas as pl
from jax.experimental.pallas import tpu as pltpu
from jax.sharding import PartitionSpec as P

MESH = pl.DeviceIdType.MESH
DEPTH = 4
PLANE = 8
COLS = 256


def slots(expert_ids, experts, capacity):
    columns = jnp.arange(experts, dtype=jnp.int32)
    named = expert_ids[:, :, None] == columns[None, None, :]
    mask = jnp.any(named, axis=1)
    rows = jnp.arange(expert_ids.shape[0], dtype=jnp.int32)
    earlier = (rows[None, :] < rows[:, None]).astype(jnp.bfloat16)
    rank = jnp.dot(earlier, mask.astype(jnp.bfloat16), preferred_element_type=jnp.float32)
    rank = rank.astype(jnp.int32)
    masked = jnp.where(mask, rank, -1)
    places = jnp.arange(capacity, dtype=jnp.int32)
    chooser = (masked.T[:, None, :] == places[None, :, None]).astype(jnp.bfloat16)
    picked = jnp.sum(jnp.where(named, rank[:, None, :], 0), axis=2)
    return chooser, expert_ids * capacity + picked


def exchange_kernel(
    tokens, chooser, weight, res, held, wv, selr, packed, outs,
    own_sem, w_sem, sel_send, sel_recv, send_sem, recv_sem, out_send, out_recv,
):
    me = lax.axis_index("expert")
    devices = held.shape[0]
    half = held.shape[1] // 2
    z = me // PLANE
    spot = lax.rem(me, PLANE)
    core = lax.rem(spot, 2)
    x = lax.rem(spot // 2, 2)
    y = spot // 4
    sib = me + 1 - 2 * core
    xn = me + 2 * (1 - 2 * x)
    yn = me + 4 * (1 - 2 * y)
    diag = 4 * (1 - 2 * y) + 2 * (1 - 2 * x)

    weight_copy = pltpu.make_async_copy(weight.at[0], wv, w_sem)
    weight_copy.start()
    own_copy = pltpu.make_async_copy(tokens, held.at[me], own_sem.at[0])
    own_copy.start()
    sel_copy = pltpu.make_async_copy(chooser.at[me], selr.at[me], own_sem.at[1])
    sel_copy.start()

    barrier = pltpu.get_barrier_semaphore()

    @pl.loop(1, devices)
    def _(d):
        pl.semaphore_signal(
            barrier, inc=1, device_id={"expert": lax.rem(me + d, devices)}, device_id_type=MESH
        )

    pl.semaphore_wait(barrier, devices - 1)
    own_copy.wait()
    sel_copy.wait()

    def sel_to(d):
        to = lax.rem(me + d, devices)
        return pltpu.make_async_remote_copy(
            src_ref=chooser.at[to], dst_ref=selr.at[me],
            send_sem=sel_send.at[to], recv_sem=sel_recv.at[me],
            device_id={"expert": to}, device_id_type=MESH,
        )

    def piece(block, h, to, index):
        part = held.at[block, pl.ds(h * half, half)]
        return pltpu.make_async_remote_copy(
            src_ref=part, dst_ref=part,
            send_sem=send_sem.at[index], recv_sem=recv_sem.at[block, h],
            device_id={"expert": to}, device_id_type=MESH,
        )

    sent = []

    def send(block, h, to, when=None):
        copy = piece(block, h, to, len(sent))
        if when is None:
            copy.start()
        else:
            pl.when(when)(copy.start)
        sent.append((copy, when))

    def arrived(block, h):
        piece(block, h, sib, 0).wait_recv()

    upper = z // 2
    mirrored = z + upper * (3 - 2 * z)

    def plane(t):
        order = t + mirrored * (1 - 2 * t) if t < 2 else t
        return order + upper * (3 - 2 * order)

    def base(t):
        return plane(t) * PLANE

    def stage_a(t):
        block, level = base(t) + spot, plane(t)
        for h in (0, 1):
            if t > 0:
                arrived(block, h)
            send(block, h, lax.rem(me + PLANE, devices),
                 jnp.logical_and(z < DEPTH - 1, level <= z))
            send(block, h, lax.rem(me + devices - PLANE, devices),
                 jnp.logical_and(z > 0, level >= z))
            send(block, h, (xn, yn)[h])
        for h in (0, 1):
            send(block, h, (yn, xn)[h])
            send(block, h, sib)

    def stage_b(t):
        for h, near, to in ((0, xn, yn), (1, yn, xn)):
            block = base(t) + lax.rem(near, PLANE)
            arrived(block, h)
            send(block, h, to)
            send(block, h, sib)

    def stage_c(t):
        across = base(t) + spot + diag
        for block, h in (
            (base(t) + lax.rem(yn, PLANE), 0), (base(t) + lax.rem(xn, PLANE), 1),
            (across, 0), (across, 1),
        ):
            arrived(block, h)
            send(block, h, sib)

    def out_to(s):
        return pltpu.make_async_remote_copy(
            src_ref=outs.at[s], dst_ref=res.at[me],
            send_sem=out_send.at[s], recv_sem=out_recv.at[me],
            device_id={"expert": s}, device_id_type=MESH,
        )

    cap = selr.shape[1]

    def stage_d(t):
        first = base(t)
        for q in range(4):
            for h in (0, 1):
                arrived(first + 2 * q + (1 - core), h)

        @pl.loop(0, PLANE)
        def _(q):
            s = first + q

            @pl.when(s != me)
            def _():
                pltpu.make_async_remote_copy(
                    src_ref=chooser.at[s], dst_ref=selr.at[s],
                    send_sem=sel_send.at[s], recv_sem=sel_recv.at[s],
                    device_id={"expert": sib}, device_id_type=MESH,
                ).wait_recv()

            rows = pl.ds(pl.multiple_of(q * cap, 16), cap)
            packed[rows, :] = jnp.dot(
                selr[s], held[s], preferred_element_type=jnp.float32
            ).astype(jnp.bfloat16)

        if t == 1:
            weight_copy.wait()

        @pl.loop(0, wv.shape[1] // COLS)
        def _(j):
            columns = pl.ds(pl.multiple_of(j * COLS, COLS), COLS)
            v = jnp.dot(packed[...], wv[:, columns], preferred_element_type=jnp.float32)
            act = (v / (1.0 + jnp.exp(-v))).astype(jnp.bfloat16)
            outs[pl.ds(first, PLANE), :, columns] = act.reshape(PLANE, cap, COLS)


    def send_out(t):
        first = base(t)

        @pl.loop(0, PLANE)
        def _(q):
            s = first + lax.rem(spot + q, PLANE)

            @pl.when(s != me)
            def _():
                out_to(s).start()

            @pl.when(s == me)
            def _():
                pltpu.make_async_copy(outs.at[me], res.at[me], own_sem.at[2]).start()

    stage_a(0)

    @pl.loop(1, devices)
    def _(d):
        sel_to(d).start()

    stage_b(0)
    stage_a(1)
    stage_b(1)
    stage_c(0)
    stage_a(2)
    stage_b(2)
    stage_c(1)
    stage_a(3)
    stage_d(1)
    send_out(1)
    stage_c(2)
    stage_d(2)
    send_out(2)
    stage_b(3)
    stage_d(0)
    stage_c(3)
    stage_d(3)
    send_out(3)
    send_out(0)

    for copy, when in sent:
        if when is None:
            copy.wait_send()
        else:
            pl.when(when)(copy.wait_send)

    @pl.loop(1, devices)
    def _(d):
        sel_to(d).wait_send()
        s = lax.rem(me + d, devices)
        out_to(s).wait_send()
        pltpu.make_async_remote_copy(
            src_ref=outs.at[s], dst_ref=res.at[s],
            send_sem=out_send.at[s], recv_sem=out_recv.at[s],
            device_id={"expert": s}, device_id_type=MESH,
        ).wait_recv()

    pltpu.make_async_copy(outs.at[me], res.at[me], own_sem.at[2]).wait()


def exchange(tokens, chooser, weight):
    rows, model_width = tokens.shape
    devices, capacity, _ = chooser.shape
    hidden = weight.shape[2]
    sends = 22 * DEPTH
    anywhere = pl.BlockSpec(memory_space=pl.ANY)
    return pl.pallas_call(
        exchange_kernel,
        out_shape=jax.ShapeDtypeStruct((devices, capacity, hidden), jnp.bfloat16),
        in_specs=[anywhere, pl.BlockSpec(memory_space=pltpu.VMEM), anywhere],
        out_specs=anywhere,
        scratch_shapes=[
            pltpu.VMEM((devices, rows, model_width), jnp.bfloat16),
            pltpu.VMEM((model_width, hidden), jnp.bfloat16),
            pltpu.VMEM((devices, capacity, rows), jnp.bfloat16),
            pltpu.VMEM((PLANE * capacity, model_width), jnp.bfloat16),
            pltpu.VMEM((devices, capacity, hidden), jnp.bfloat16),
            pltpu.SemaphoreType.DMA((3,)),
            pltpu.SemaphoreType.DMA,
            pltpu.SemaphoreType.DMA((devices,)),
            pltpu.SemaphoreType.DMA((devices,)),
            pltpu.SemaphoreType.DMA((sends,)),
            pltpu.SemaphoreType.DMA((devices, 2)),
            pltpu.SemaphoreType.DMA((devices,)),
            pltpu.SemaphoreType.DMA((devices,)),
        ],
        compiler_params=pltpu.CompilerParams(
            collective_id=0, has_side_effects=True, vmem_limit_bytes=56 * 1024 * 1024
        ),
    )(tokens, chooser, weight)


def body(tokens, expert_ids, route_weight, expert_weight):
    tok_rows, picks = expert_ids.shape
    per_device, model_width, hidden = expert_weight.shape
    devices = lax.axis_size("expert")
    experts = per_device * devices
    small_cap = (tok_rows * picks + experts - 1) // experts
    capacity = max(small_cap + 1, small_cap + small_cap // 2)
    chooser, place = slots(expert_ids, experts, capacity)
    if devices == DEPTH * PLANE and per_device == 1 and lax.axis_size("group") == 1:
        results = exchange(tokens, chooser, expert_weight)
    else:
        packed = jnp.dot(
            chooser.reshape(experts * capacity, tok_rows), tokens,
            preferred_element_type=jnp.float32,
        ).astype(jnp.bfloat16).reshape(experts, capacity, model_width)
        received = lax.all_to_all(packed, "expert", split_axis=0, concat_axis=0, tiled=True)
        grouped = received.reshape(devices, per_device, capacity, model_width)
        preact = jnp.einsum(
            "necd,edf->necf", grouped, expert_weight, preferred_element_type=jnp.float32
        )
        activated = jax.nn.silu(preact).astype(jnp.bfloat16).reshape(experts, capacity, hidden)
        results = lax.all_to_all(activated, "expert", split_axis=0, concat_axis=0, tiled=True)
    positions = jnp.arange(experts * capacity, dtype=jnp.int32)
    finder = (place.reshape(-1, 1) == positions[None, :]).astype(jnp.bfloat16)
    gathered = jnp.dot(
        finder, results.reshape(experts * capacity, hidden), preferred_element_type=jnp.float32
    )
    routed = route_weight.reshape(-1, 1) * gathered
    return routed.astype(jnp.bfloat16).reshape(tok_rows, picks, hidden)


def solution(mesh):
    in_specs = (
        P(("group", "expert"), None),
        P(("group", "expert"), None),
        P(("group", "expert"), None),
        P("expert", None, None),
    )
    out_specs = P(("group", "expert"), None, None)
    return jax.shard_map(body, mesh=mesh, in_specs=in_specs, out_specs=out_specs, check_vma=False)
```
